32 devices in a mesh: parts: 2 (over y), ckpt: 4 (over x, core), dp: 4 (over z).
Axes of the slice: x: 2, y: 2, z: 4, core: 2. Of those that a mesh axis runs over, the one named last changes fastest.
Arguments:
- train_grads: bfloat16 [4, 8192, 4096], P('ckpt', ('parts', 'dp')), parts along dimension 1, may hold values from -6 to 6
- query_slots: bfloat16 [4, 4, 256, 4096], P('ckpt', 'dp'), may hold values from -0.09375 to 0.09375
- owners: int32 [4], replicated, may hold values from 0 to 3, as said below
- lr_weights: float32 [4], P('ckpt'), may hold values from 0.3 to 3
Outputs:
- scores: float32 [1024, 8192], P('ckpt', ('parts', 'dp')), parts along dimension 1
The draws below stay inside these ranges and needn't reach their ends.
There are 2 independent parts, one for each index of `parts`. The reference program is written for one: setup_inputs(seed, part) draws one part's arguments, and reference() takes and returns one part's arrays. A program takes and returns all parts, laid end to end along the dimension named above; an argument that names none is the same for every part. Nothing has to cross between parts.
Inputs may be any that keep to these rules, and one draw needn't show every extreme that they name: The 4 owners are distinct.
All inputs are finite; a program needn't handle non-finite values.
Results may differ from the reference program's by a relative error of at most 0.0003.
Values may be sent and summed in bfloat16 or wider, within the bound.
A program may use at most 128 MiB of HBM per device.

```python
import math
import jax
import jax.numpy as jnp
from jax import lax

K = 4096
QUERIES = 1024
GROUPS = 4
QCH = 256
NTRAIN = 4096
NCK = 4
N_DP = 4


def draw_owners(key, part):
    key = jax.random.fold_in(key, 11)
    order = jax.random.permutation(key, N_DP)
    return order[:GROUPS].astype(jnp.int32)


def level_of(stream_key, extent, cuts, low, largest):
    def one(dim, parts):
        steps = jax.random.uniform(jax.random.fold_in(jax.random.fold_in(stream_key, 6), dim), (parts,), jnp.float32, low / len(cuts), largest / len(cuts))
        return jnp.repeat(jnp.exp(steps), extent[dim] // parts).reshape((-1,) + (1,) * (len(extent) - dim - 1))

    loudness = one(*cuts[0])
    for cut in cuts[1:]:
        loudness = loudness * one(*cut)
    return loudness


def gaussian(stream_key, extent, scale, most, cuts=(), kind=jnp.bfloat16):
    level = level_of(stream_key, extent, cuts, -0.22, 0.18) if cuts else 1.0
    drawn = jax.random.normal(stream_key, extent, jnp.float32) * scale * level
    return jnp.minimum(jnp.maximum(drawn, -most), most).astype(kind)


def setup_inputs(seed: int = 0, part: int = 0) -> dict:
    seeds = jax.random.split(jax.random.key(seed), 5)
    part_keys = jax.random.split(jax.random.fold_in(seeds[4], part), 5)
    return {
        "train_grads": gaussian(part_keys[0], (NCK, NTRAIN, K), 1.0, 6.0, ((0, 4), (1, 4))),
        "query_slots": gaussian(seeds[1], (NCK, N_DP, QCH, K), K ** -0.5, 0.09375, ((0, 4), (1, 4))),
        "owners": draw_owners(jax.random.fold_in(seeds[4], 71), part),
        "lr_weights": jnp.clip(jnp.exp(math.log(3.0) - 2.3025851 * jax.random.uniform(seeds[3], (NCK,), jnp.float32) ** level_of(seeds[3], (NCK,), ((0, 4),), -0.2, 0.2)), 0.3, 3.0),
    }


def reference(train_grads, query_slots, owners, lr_weights):
    def one_ckpt(total, index):
        slots = query_slots[index]
        queries = jnp.concatenate([slots[owners[r]] for r in range(GROUPS)], axis=0)
        term = lax.dot_general(queries, train_grads[index], (((1,), (1,)), ((), ())), preferred_element_type=jnp.float32)
        return total + lr_weights[index] * term, None

    start = jnp.zeros((QUERIES, NTRAIN), jnp.float32)
    total, _ = lax.scan(one_ckpt, start, jnp.arange(NCK))
    return total
```

```python
import functools

import jax
import jax.numpy as jnp
from jax import lax
from jax.experimental import pallas as pl
from jax.experimental.pallas import tpu as pltpu
from jax.sharding import PartitionSpec as P

GROUPS = 4
CHUNK = 32
MESH = pl.DeviceIdType.MESH


def from_root(block, axis, holder):
    block = jnp.where(lax.axis_index(axis) == holder, block, jnp.zeros_like(block))
    return lax.psum(block, axis)


def weighted_scores(block, grads, weight):
    product = lax.dot_general(
        block, grads, (((1,), (1,)), ((), ())), preferred_element_type=jnp.float32
    )
    return weight * product


def per_device(train_grads, query_slots, owners, lr_weights):
    grads = train_grads[0]
    slot = query_slots[0, 0]
    weight = lr_weights[0]
    blocks = []
    for step in range(GROUPS):
        blocks.append(from_root(slot, "dp", owners[step]))
    queries = jnp.concatenate(blocks, axis=0)
    term = weighted_scores(queries, grads, weight)
    return lax.psum_scatter(term, "ckpt", scatter_dimension=0, tiled=True)


def slot_kernel(
    grads_hbm, slot_hbm, weight_ref, out_ref,
    q, g, term, core_in, pair, x_in, final,
    load_sem, right_sem, left_sem, z_sem, y_send, y_sem,
    a_send, a_recv, b_send, b_recv, c_send, c_recv, store_sem,
):
    slots, rows, _ = q.shape
    half = term.shape[-1]
    chunks = rows // (2 * CHUNK)
    steps = (slots - 1) * chunks
    y, j, z = lax.axis_index("parts"), lax.axis_index("ckpt"), lax.axis_index("dp")
    x, c = lax.div(j, 2), lax.rem(j, 2)
    other_y = {"parts": 1 - y}
    other_core = {"ckpt": 2 * x + 1 - c}
    other_x = {"ckpt": 2 * (1 - x) + c}
    right, left = {"dp": z + 1}, {"dp": z - 1}
    has_right, has_left = z < slots - 1, z > 0

    def loads():
        return (
            pltpu.make_async_copy(slot_hbm, q.at[z], load_sem.at[0]),
            pltpu.make_async_copy(grads_hbm, g, load_sem.at[1]),
        )

    def sent(i, of):
        return pl.ds(pl.multiple_of(i * 2 * CHUNK + of * CHUNK, CHUNK), CHUNK)

    def remote(src, dst, send, recv, device):
        return pltpu.make_async_remote_copy(
            src_ref=src, dst_ref=dst, send_sem=send, recv_sem=recv, device_id=device, device_id_type=MESH
        )

    def to_right(s, i, src=None):
        block = q.at[s, sent(i, y)]
        return remote(block if src is None else src, block, right_sem.at[s, i], z_sem.at[s, i], right)

    def to_left(s, i, src=None):
        block = q.at[s, sent(i, y)]
        return remote(block if src is None else src, block, left_sem.at[s, i], z_sem.at[s, i], left)

    def to_y(s, i):
        block = q.at[s, sent(i, y)]
        return remote(block, block, y_send.at[s, i], y_sem.at[s, i], other_y)

    far = lax.div(z, 2)
    near = z + far * (slots - 1 - 2 * z)

    def slot_of(p):
        k = lax.div(p, chunks) + 1
        later = lax.div(k + 2, 4)
        f = (1 - later) * (1 - near) + later * k
        return f + far * (slots - 1 - 2 * f)

    def place(p):
        if isinstance(p, int):
            return z, slice(None), 0
        i = lax.rem(p, chunks)
        return slot_of(p), pl.ds(pl.multiple_of(i * 2 * CHUNK, 2 * CHUNK), 2 * CHUNK), p + 1

    def core_copy(p):
        s, r, n = place(p)
        return remote(term.at[s, 1 - c, r], core_in.at[s, r], a_send.at[n], a_recv.at[n], other_core)

    def x_copy(p):
        s, r, n = place(p)
        return remote(pair.at[s, r], x_in.at[s, r], b_send.at[n], b_recv.at[n], other_x)

    def final_copies(p):
        s, r, n = place(p)
        mine = pl.ds(pl.multiple_of(c * half, half), half)
        dst = out_ref.at[s, r, mine]
        return (
            remote(final.at[s, r], dst, c_send.at[n], c_recv.at[n], other_core),
            pltpu.make_async_copy(final.at[s, r], dst, store_sem.at[n]),
        )

    def arrived_final(p):
        s, r, n = place(p)
        theirs = pl.ds(pl.multiple_of((1 - c) * half, half), half)
        return remote(final.at[s, r], out_ref.at[s, r, theirs], c_send.at[n], c_recv.at[n], other_core)

    def multiply(p):
        s, r, _ = place(p)
        for step in range(2):
            h = (1 - c) if step == 0 else c
            columns = pl.ds(pl.multiple_of(h * half, half), half)
            product = lax.dot_general(
                q[s, r], g[columns], (((1,), (1,)), ((), ())), preferred_element_type=jnp.float32
            )
            term[s, h, r] = weight_ref[0] * product
            if step == 0:
                core_copy(p).start()

    def add_core(p):
        s, r, _ = place(p)
        core_copy(p).wait_recv()
        pair[s, r] = term[s, c, r] + core_in[s, r]
        x_copy(p).start()

    def add_x(p):
        s, r, _ = place(p)
        x_copy(p).wait_recv()
        final[s, r] = pair[s, r] + x_in[s, r]
        for copy in final_copies(p):
            copy.start()

    for load in loads():
        load.start()

    barrier = pltpu.get_barrier_semaphore()
    for device in (other_y, other_core, other_x):
        pl.semaphore_signal(barrier, inc=1, device_id=device, device_id_type=MESH)
    for has, device in ((has_right, right), (has_left, left)):

        @pl.when(has)
        def _():
            pl.semaphore_signal(barrier, inc=1, device_id=device, device_id_type=MESH)

    pl.semaphore_wait(barrier, 3 + lax.div(z + slots - 1, slots) + 1 - lax.div(z + 1, slots))

    for i in range(chunks):
        src = slot_hbm.at[sent(i, y)]

        @pl.when(has_right)
        def _():
            to_right(z, i, src).start()

        @pl.when(has_left)
        def _():
            to_left(z, i, src).start()

    def forward(n):
        t, i = lax.div(n, chunks), lax.rem(n, chunks)

        @pl.when(z - 1 - t >= 0)
        def _():
            s = z - 1 - t
            to_right(s, i).wait_recv()
            to_y(s, i).start()

            @pl.when(has_right)
            def _():
                to_right(s, i).start()

        @pl.when(z + 1 + t < slots)
        def _():
            s = z + 1 + t
            to_left(s, i).wait_recv()
            to_y(s, i).start()

            @pl.when(has_left)
            def _():
                to_left(s, i).start()

    forward(jnp.int32(0))
    for load in loads():
        load.wait()
    multiply(-1)

    def body(n, carry):
        @pl.when(n < steps)
        def _():
            forward(n)

        @pl.when(n == 1)
        def _():
            add_core(-1)

        @pl.when(n == 2)
        def _():
            add_x(-1)

        @pl.when(n <= steps)
        def _():
            p = n - 1
            to_y(slot_of(p), lax.rem(p, chunks)).wait_recv()
            multiply(p)

        @pl.when(jnp.logical_and(n >= 2, n <= steps + 1))
        def _():
            add_core(n - 2)

        @pl.when(n >= 3)
        def _():
            add_x(n - 3)

        return carry

    lax.fori_loop(1, steps + 3, body, 0)

    def finish(p):
        core_copy(p).wait_send()
        x_copy(p).wait_send()
        arrived_final(p).wait_recv()
        sent_copy, stored = final_copies(p)
        sent_copy.wait_send()
        stored.wait()

    finish(-1)

    def finish_step(p, carry):
        to_y(slot_of(p), lax.rem(p, chunks)).wait_send()
        finish(p)
        return carry

    lax.fori_loop(0, steps, finish_step, 0)

    def finish_sends(n, carry):
        s, i = lax.div(n, chunks), lax.rem(n, chunks)

        @pl.when(jnp.logical_and(has_right, s <= z))
        def _():
            to_right(s, i).wait_send()

        @pl.when(jnp.logical_and(has_left, s >= z))
        def _():
            to_left(s, i).wait_send()

        return carry

    lax.fori_loop(0, slots * chunks, finish_sends, 0)


def all_slots_owned(train_grads, query_slots, owners, lr_weights):
    grads, slot = train_grads[0], query_slots[0, 0]
    slots = GROUPS
    rows, depth = slot.shape
    columns = grads.shape[0]
    chunks = rows // (2 * CHUNK)
    items = (slots - 1) * chunks + 1
    dma = pltpu.SemaphoreType.DMA
    f32 = jnp.float32
    scores = pl.pallas_call(
        slot_kernel,
        out_shape=jax.ShapeDtypeStruct((slots, rows, columns), f32),
        in_specs=[
            pl.BlockSpec(memory_space=pl.ANY),
            pl.BlockSpec(memory_space=pl.ANY),
            pl.BlockSpec(memory_space=pltpu.SMEM),
        ],
        out_specs=pl.BlockSpec(memory_space=pl.ANY),
        scratch_shapes=[
            pltpu.VMEM((slots, rows, depth), slot.dtype),
            pltpu.VMEM((columns, depth), grads.dtype),
            pltpu.VMEM((slots, 2, rows, columns // 2), f32),
            pltpu.VMEM((slots, rows, columns // 2), f32),
            pltpu.VMEM((slots, rows, columns // 2), f32),
            pltpu.VMEM((slots, rows, columns // 2), f32),
            pltpu.VMEM((slots, rows, columns // 2), f32),
            dma((2,)),
            dma((slots, chunks)),
            dma((slots, chunks)),
            dma((slots, chunks)),
            dma((slots, chunks)),
            dma((slots, chunks)),
            dma((items,)),
            dma((items,)),
            dma((items,)),
            dma((items,)),
            dma((items,)),
            dma((items,)),
            dma((items,)),
        ],
        compiler_params=pltpu.CompilerParams(
            collective_id=0, has_side_effects=True, vmem_limit_bytes=56 * 1024 * 1024
        ),
        cost_estimate=pl.CostEstimate(
            flops=2 * slots * rows * columns * depth, bytes_accessed=16 << 20, transcendentals=0
        ),
    )(grads, slot, lr_weights)
    return lax.dynamic_index_in_dim(scores, owners[lax.axis_index("ckpt")], 0, keepdims=False)


def solution(mesh):
    placed = (P("ckpt", ("parts", "dp"), None), P("ckpt", "dp", None, None), P(), P("ckpt"))
    sizes = dict(mesh.shape)
    every = sizes["dp"] == GROUPS and sizes["ckpt"] == GROUPS and sizes["parts"] == 2
    return jax.shard_map(
        all_slots_owned if every else per_device,
        mesh=mesh,
        in_specs=placed,
        out_specs=P("ckpt", ("parts", "dp")),
        check_vma=False,
    )
```

```python
import functools

import jax
import jax.numpy as jnp
from jax import lax
from jax.experimental import pallas as pl
from jax.experimental.pallas import tpu as pltpu
from jax.sharding import PartitionSpec as P

GROUPS = 4
CHUNK = 32
TURN = 256
LAG_Y = 2
LAG_CORE = 2
LAG_X = 2
MESH = pl.DeviceIdType.MESH


def from_root(block, axis, holder):
    block = jnp.where(lax.axis_index(axis) == holder, block, jnp.zeros_like(block))
    return lax.psum(block, axis)


def weighted_scores(block, grads, weight):
    product = lax.dot_general(
        block, grads, (((1,), (1,)), ((), ())), preferred_element_type=jnp.float32
    )
    return weight * product


def per_device(train_grads, query_slots, owners, lr_weights):
    grads = train_grads[0]
    slot = query_slots[0, 0]
    weight = lr_weights[0]
    blocks = []
    for step in range(GROUPS):
        blocks.append(from_root(slot, "dp", owners[step]))
    queries = jnp.concatenate(blocks, axis=0)
    term = weighted_scores(queries, grads, weight)
    return lax.psum_scatter(term, "ckpt", scatter_dimension=0, tiled=True)


def slot_kernel(
    grads_hbm, slot_hbm, weight_ref, out_ref,
    q, g, gt, term, core_in, pair, x_in, final,
    load_sem, right_sem, left_sem, z_sem, y_send, y_sem,
    a_send, a_recv, b_send, b_recv, c_send, c_recv, store_sem,
):
    slots, rows, _ = q.shape
    half = term.shape[-1]
    chunks = rows // (2 * CHUNK)
    steps = (slots - 1) * chunks
    y, j, z = lax.axis_index("parts"), lax.axis_index("ckpt"), lax.axis_index("dp")
    x, c = lax.div(j, 2), lax.rem(j, 2)
    other_y = {"parts": 1 - y}
    other_core = {"ckpt": 2 * x + 1 - c}
    other_x = {"ckpt": 2 * (1 - x) + c}
    right, left = {"dp": z + 1}, {"dp": z - 1}
    has_right, has_left = z < slots - 1, z > 0

    def loads():
        return (
            pltpu.make_async_copy(slot_hbm, q.at[z], load_sem.at[0]),
            pltpu.make_async_copy(grads_hbm, g, load_sem.at[1]),
        )

    def sent(i, of):
        return pl.ds(pl.multiple_of(i * 2 * CHUNK + of * CHUNK, CHUNK), CHUNK)

    def remote(src, dst, send, recv, device):
        return pltpu.make_async_remote_copy(
            src_ref=src, dst_ref=dst, send_sem=send, recv_sem=recv, device_id=device, device_id_type=MESH
        )

    def to_right(s, i, src=None):
        block = q.at[s, sent(i, y)]
        return remote(block if src is None else src, block, right_sem.at[s, i], z_sem.at[s, i], right)

    def to_left(s, i, src=None):
        block = q.at[s, sent(i, y)]
        return remote(block if src is None else src, block, left_sem.at[s, i], z_sem.at[s, i], left)

    def to_y(s, i):
        block = q.at[s, sent(i, y)]
        return remote(block, block, y_send.at[s, i], y_sem.at[s, i], other_y)

    far = lax.div(z, 2)
    near = z + far * (slots - 1 - 2 * z)

    def slot_of(p):
        k = lax.div(p, chunks) + 1
        later = lax.div(k + 2, 4)
        f = (1 - later) * (1 - near) + later * k
        return f + far * (slots - 1 - 2 * f)

    def place(p):
        if isinstance(p, int):
            return z, slice(None), 0
        i = lax.rem(p, chunks)
        return slot_of(p), pl.ds(pl.multiple_of(i * 2 * CHUNK, 2 * CHUNK), 2 * CHUNK), p + 1

    def core_copy(p):
        s, r, n = place(p)
        return remote(term.at[s, 1 - c, r], core_in.at[s, r], a_send.at[n], a_recv.at[n], other_core)

    def x_copy(p):
        s, r, n = place(p)
        return remote(pair.at[s, r], x_in.at[s, r], b_send.at[n], b_recv.at[n], other_x)

    def final_copies(p):
        s, r, n = place(p)
        mine = pl.ds(pl.multiple_of(c * half, half), half)
        dst = out_ref.at[s, r, mine]
        return (
            remote(final.at[s, r], dst, c_send.at[n], c_recv.at[n], other_core),
            pltpu.make_async_copy(final.at[s, r], dst, store_sem.at[n]),
        )

    def arrived_final(p):
        s, r, n = place(p)
        theirs = pl.ds(pl.multiple_of((1 - c) * half, half), half)
        return remote(final.at[s, r], out_ref.at[s, r, theirs], c_send.at[n], c_recv.at[n], other_core)

    def multiply(p):
        s, r, _ = place(p)
        for step in range(2):
            h = (1 - c) if step == 0 else c
            columns = pl.ds(pl.multiple_of(h * half, half), half)
            product = lax.dot_general(
                q[s, r], gt[:, columns], (((1,), (0,)), ((), ())), preferred_element_type=jnp.float32
            )
            term[s, h, r] = weight_ref[0] * product
            if step == 0:
                core_copy(p).start()

    def add_core(p):
        s, r, _ = place(p)
        core_copy(p).wait_recv()
        pair[s, r] = term[s, c, r] + core_in[s, r]
        x_copy(p).start()

    def add_x(p):
        s, r, _ = place(p)
        x_copy(p).wait_recv()
        final[s, r] = pair[s, r] + x_in[s, r]
        for copy in final_copies(p):
            copy.start()

    for load in loads():
        load.start()

    barrier = pltpu.get_barrier_semaphore()
    for device in (other_y, other_core, other_x):
        pl.semaphore_signal(barrier, inc=1, device_id=device, device_id_type=MESH)
    for has, device in ((has_right, right), (has_left, left)):

        @pl.when(has)
        def _():
            pl.semaphore_signal(barrier, inc=1, device_id=device, device_id_type=MESH)

    pl.semaphore_wait(barrier, 3 + lax.div(z + slots - 1, slots) + 1 - lax.div(z + 1, slots))

    for i in range(chunks):
        src = slot_hbm.at[sent(i, y)]

        @pl.when(has_right)
        def _():
            to_right(z, i, src).start()

        @pl.when(has_left)
        def _():
            to_left(z, i, src).start()

    def forward(n):
        t, i = lax.div(n, chunks), lax.rem(n, chunks)

        @pl.when(z - 1 - t >= 0)
        def _():
            s = z - 1 - t
            to_right(s, i).wait_recv()
            to_y(s, i).start()

            @pl.when(has_right)
            def _():
                to_right(s, i).start()

        @pl.when(z + 1 + t < slots)
        def _():
            s = z + 1 + t
            to_left(s, i).wait_recv()
            to_y(s, i).start()

            @pl.when(has_left)
            def _():
                to_left(s, i).start()

    forward(jnp.int32(0))
    for load in loads():
        load.wait()

    def turn(b, carry):
        r = pl.ds(pl.multiple_of(b * TURN, TURN), TURN)
        gt[:, r] = g[r].T
        return carry

    lax.fori_loop(0, g.shape[0] // TURN, turn, 0)
    multiply(-1)

    def body(n, carry):
        @pl.when(n < steps)
        def _():
            forward(n)

        @pl.when(n == 2)
        def _():
            add_core(-1)

        @pl.when(n == 4)
        def _():
            add_x(-1)

        @pl.when(jnp.logical_and(n >= LAG_Y, n < LAG_Y + steps))
        def _():
            p = n - LAG_Y
            to_y(slot_of(p), lax.rem(p, chunks)).wait_recv()
            multiply(p)

        @pl.when(jnp.logical_and(n >= LAG_Y + LAG_CORE, n < LAG_Y + LAG_CORE + steps))
        def _():
            add_core(n - LAG_Y - LAG_CORE)

        @pl.when(n >= LAG_Y + LAG_CORE + LAG_X)
        def _():
            add_x(n - LAG_Y - LAG_CORE - LAG_X)

        return carry

    lax.fori_loop(1, steps + LAG_Y + LAG_CORE + LAG_X, body, 0)

    def finish(p):
        core_copy(p).wait_send()
        x_copy(p).wait_send()
        arrived_final(p).wait_recv()
        sent_copy, stored = final_copies(p)
        sent_copy.wait_send()
        stored.wait()

    finish(-1)

    def finish_step(p, carry):
        to_y(slot_of(p), lax.rem(p, chunks)).wait_send()
        finish(p)
        return carry

    lax.fori_loop(0, steps, finish_step, 0)

    def finish_sends(n, carry):
        s, i = lax.div(n, chunks), lax.rem(n, chunks)

        @pl.when(jnp.logical_and(has_right, s <= z))
        def _():
            to_right(s, i).wait_send()

        @pl.when(jnp.logical_and(has_left, s >= z))
        def _():
            to_left(s, i).wait_send()

        return carry

    lax.fori_loop(0, slots * chunks, finish_sends, 0)


def all_slots_owned(train_grads, query_slots, owners, lr_weights):
    grads, slot = train_grads[0], query_slots[0, 0]
    slots = GROUPS
    rows, depth = slot.shape
    columns = grads.shape[0]
    chunks = rows // (2 * CHUNK)
    items = (slots - 1) * chunks + 1
    dma = pltpu.SemaphoreType.DMA
    f32 = jnp.float32
    scores = pl.pallas_call(
        slot_kernel,
        out_shape=jax.ShapeDtypeStruct((slots, rows, columns), f32),
        in_specs=[
            pl.BlockSpec(memory_space=pl.ANY),
            pl.BlockSpec(memory_space=pl.ANY),
            pl.BlockSpec(memory_space=pltpu.SMEM),
        ],
        out_specs=pl.BlockSpec(memory_space=pl.ANY),
        scratch_shapes=[
            pltpu.VMEM((slots, rows, depth), slot.dtype),
            pltpu.VMEM((columns, depth), grads.dtype),
            pltpu.VMEM((depth, columns), grads.dtype),
            pltpu.VMEM((slots, 2, rows, columns // 2), f32),
            pltpu.VMEM((slots, rows, columns // 2), f32),
            pltpu.VMEM((slots, rows, columns // 2), f32),
            pltpu.VMEM((slots, rows, columns // 2), f32),
            pltpu.VMEM((slots, rows, columns // 2), f32),
            dma((2,)),
            dma((slots, chunks)),
            dma((slots, chunks)),
            dma((slots, chunks)),
            dma((slots, chunks)),
            dma((slots, chunks)),
            dma((items,)),
            dma((items,)),
            dma((items,)),
            dma((items,)),
            dma((items,)),
            dma((items,)),
            dma((items,)),
        ],
        compiler_params=pltpu.CompilerParams(
            collective_id=0, has_side_effects=True, vmem_limit_bytes=56 * 1024 * 1024
        ),
        cost_estimate=pl.CostEstimate(
            flops=2 * slots * rows * columns * depth, bytes_accessed=16 << 20, transcendentals=0
        ),
    )(grads, slot, lr_weights)
    return lax.dynamic_index_in_dim(scores, owners[lax.axis_index("ckpt")], 0, keepdims=False)


def solution(mesh):
    placed = (P("ckpt", ("parts", "dp"), None), P("ckpt", "dp", None, None), P(), P("ckpt"))
    sizes = dict(mesh.shape)
    every = sizes["dp"] == GROUPS and sizes["ckpt"] == GROUPS and sizes["parts"] == 2
    return jax.shard_map(
        all_slots_owned if every else per_device,
        mesh=mesh,
        in_specs=placed,
        out_specs=P("ckpt", ("parts", "dp")),
        check_vma=False,
    )
```

```python
import functools

import jax
import jax.numpy as jnp
from jax import lax
from jax.experimental import pallas as pl
from jax.experimental.pallas import tpu as pltpu
from jax.sharding import PartitionSpec as P

GROUPS = 4
CHUNK = 32
TURN = 256
LAG_Y = 2
LAG_CORE = 2
LAG_X = 2
MESH = pl.DeviceIdType.MESH


def from_root(block, axis, holder):
    block = jnp.where(lax.axis_index(axis) == holder, block, jnp.zeros_like(block))
    return lax.psum(block, axis)


def weighted_scores(block, grads, weight):
    product = lax.dot_general(
        block, grads, (((1,), (1,)), ((), ())), preferred_element_type=jnp.float32
    )
    return weight * product


def per_device(train_grads, query_slots, owners, lr_weights):
    grads = train_grads[0]
    slot = query_slots[0, 0]
    weight = lr_weights[0]
    blocks = []
    for step in range(GROUPS):
        blocks.append(from_root(slot, "dp", owners[step]))
    queries = jnp.concatenate(blocks, axis=0)
    term = weighted_scores(queries, grads, weight)
    return lax.psum_scatter(term, "ckpt", scatter_dimension=0, tiled=True)


def slot_kernel(
    grads_hbm, slot_hbm, weight_ref, out_ref,
    q, g, gt, term, core_in, pair, x_in, final,
    load_sem, right_sem, left_sem, z_sem, y_send, y_sem,
    a_send, a_recv, b_send, b_recv, c_send, c_recv, store_sem,
):
    slots, rows, _ = q.shape
    half = term.shape[-1]
    chunks = rows // (2 * CHUNK)
    steps = (slots - 1) * chunks
    y, j, z = lax.axis_index("parts"), lax.axis_index("ckpt"), lax.axis_index("dp")
    x, c = lax.div(j, 2), lax.rem(j, 2)
    other_y = {"parts": 1 - y}
    other_core = {"ckpt": 2 * x + 1 - c}
    other_x = {"ckpt": 2 * (1 - x) + c}
    right, left = {"dp": z + 1}, {"dp": z - 1}
    has_right, has_left = z < slots - 1, z > 0

    def loads():
        return (
            pltpu.make_async_copy(slot_hbm, q.at[z], load_sem.at[0]),
            pltpu.make_async_copy(grads_hbm, g, load_sem.at[1]),
        )

    def sent(i, of):
        return pl.ds(pl.multiple_of(i * 2 * CHUNK + of * CHUNK, CHUNK), CHUNK)

    def remote(src, dst, send, recv, device):
        return pltpu.make_async_remote_copy(
            src_ref=src, dst_ref=dst, send_sem=send, recv_sem=recv, device_id=device, device_id_type=MESH
        )

    def to_right(s, i, src=None):
        block = q.at[s, sent(i, y)]
        return remote(block if src is None else src, block, right_sem.at[s, i], z_sem.at[s, i], right)

    def to_left(s, i, src=None):
        block = q.at[s, sent(i, y)]
        return remote(block if src is None else src, block, left_sem.at[s, i], z_sem.at[s, i], left)

    def to_y(s, i):
        block = q.at[s, sent(i, y)]
        return remote(block, block, y_send.at[s, i], y_sem.at[s, i], other_y)

    far = lax.div(z, 2)
    near = z + far * (slots - 1 - 2 * z)

    def slot_of(p):
        k = lax.div(p, chunks) + 1
        later = lax.div(k + 2, 4)
        f = (1 - later) * (1 - near) + later * k
        return f + far * (slots - 1 - 2 * f)

    def place(p):
        if isinstance(p, int):
            return z, slice(None), 0
        i = lax.rem(p, chunks)
        return slot_of(p), pl.ds(pl.multiple_of(i * 2 * CHUNK, 2 * CHUNK), 2 * CHUNK), p + 1

    def core_copy(p):
        s, r, n = place(p)
        return remote(term.at[s, 1 - c, r], core_in.at[s, r], a_send.at[n], a_recv.at[n], other_core)

    def x_copy(p):
        s, r, n = place(p)
        return remote(pair.at[s, r], x_in.at[s, r], b_send.at[n], b_recv.at[n], other_x)

    def final_copies(p):
        s, r, n = place(p)
        mine = pl.ds(pl.multiple_of(c * half, half), half)
        dst = out_ref.at[s, r, mine]
        return (
            remote(final.at[s, r], dst, c_send.at[n], c_recv.at[n], other_core),
            pltpu.make_async_copy(final.at[s, r], dst, store_sem.at[n]),
        )

    def arrived_final(p):
        s, r, n = place(p)
        theirs = pl.ds(pl.multiple_of((1 - c) * half, half), half)
        return remote(final.at[s, r], out_ref.at[s, r, theirs], c_send.at[n], c_recv.at[n], other_core)

    def multiply(p):
        s, r, _ = place(p)
        for step in range(2):
            h = (1 - c) if step == 0 else c
            columns = pl.ds(pl.multiple_of(h * half, half), half)
            product = lax.dot_general(
                q[s, r], gt[:, columns], (((1,), (0,)), ((), ())), preferred_element_type=jnp.float32
            )
            term[s, h, r] = weight_ref[0] * product
            if step == 0:
                core_copy(p).start()

    def add_core(p):
        s, r, _ = place(p)
        core_copy(p).wait_recv()
        pair[s, r] = term[s, c, r] + core_in[s, r]
        x_copy(p).start()

    def add_x(p):
        s, r, _ = place(p)
        x_copy(p).wait_recv()
        final[s, r] = pair[s, r] + x_in[s, r]
        for copy in final_copies(p):
            copy.start()

    for load in loads():
        load.start()

    barrier = pltpu.get_barrier_semaphore()
    for device in (other_y, other_core, other_x):
        pl.semaphore_signal(barrier, inc=1, device_id=device, device_id_type=MESH)
    for has, device in ((has_right, right), (has_left, left)):

        @pl.when(has)
        def _():
            pl.semaphore_signal(barrier, inc=1, device_id=device, device_id_type=MESH)

    pl.semaphore_wait(barrier, 3 + lax.div(z + slots - 1, slots) + 1 - lax.div(z + 1, slots))

    for i in range(chunks):
        src = slot_hbm.at[sent(i, y)]

        @pl.when(has_right)
        def _():
            to_right(z, i, src).start()

        @pl.when(has_left)
        def _():
            to_left(z, i, src).start()

    def forward(n):
        t, i = lax.div(n, chunks), lax.rem(n, chunks)

        @pl.when(z - 1 - t >= 0)
        def _():
            s = z - 1 - t
            to_right(s, i).wait_recv()
            to_y(s, i).start()

            @pl.when(has_right)
            def _():
                to_right(s, i).start()

        @pl.when(z + 1 + t < slots)
        def _():
            s = z + 1 + t
            to_left(s, i).wait_recv()
            to_y(s, i).start()

            @pl.when(has_left)
            def _():
                to_left(s, i).start()

    forward(jnp.int32(0))
    for load in loads():
        load.wait()

    def turn(b, carry):
        r = pl.ds(pl.multiple_of(b * TURN, TURN), TURN)
        gt[:, r] = g[r].T
        return carry

    lax.fori_loop(0, g.shape[0] // TURN, turn, 0)
    multiply(-1)

    def body(n, carry):
        @pl.when(n < steps)
        def _():
            forward(n)

        @pl.when(n == 2)
        def _():
            add_core(-1)

        @pl.when(n == 4)
        def _():
            add_x(-1)

        @pl.when(jnp.logical_and(n >= LAG_Y + LAG_CORE, n < LAG_Y + LAG_CORE + steps))
        def _():
            add_core(n - LAG_Y - LAG_CORE)

        @pl.when(n >= LAG_Y + LAG_CORE + LAG_X)
        def _():
            add_x(n - LAG_Y - LAG_CORE - LAG_X)

        @pl.when(jnp.logical_and(n >= LAG_Y, n < LAG_Y + steps))
        def _():
            p = n - LAG_Y
            to_y(slot_of(p), lax.rem(p, chunks)).wait_recv()
            multiply(p)

        return carry

    lax.fori_loop(1, steps + LAG_Y + LAG_CORE + LAG_X, body, 0)

    def finish(p):
        core_copy(p).wait_send()
        x_copy(p).wait_send()
        arrived_final(p).wait_recv()
        sent_copy, stored = final_copies(p)
        sent_copy.wait_send()
        stored.wait()

    finish(-1)

    def finish_step(p, carry):
        to_y(slot_of(p), lax.rem(p, chunks)).wait_send()
        finish(p)
        return carry

    lax.fori_loop(0, steps, finish_step, 0)

    def finish_sends(n, carry):
        s, i = lax.div(n, chunks), lax.rem(n, chunks)

        @pl.when(jnp.logical_and(has_right, s <= z))
        def _():
            to_right(s, i).wait_send()

        @pl.when(jnp.logical_and(has_left, s >= z))
        def _():
            to_left(s, i).wait_send()

        return carry

    lax.fori_loop(0, slots * chunks, finish_sends, 0)


def all_slots_owned(train_grads, query_slots, owners, lr_weights):
    grads, slot = train_grads[0], query_slots[0, 0]
    slots = GROUPS
    rows, depth = slot.shape
    columns = grads.shape[0]
    chunks = rows // (2 * CHUNK)
    items = (slots - 1) * chunks + 1
    dma = pltpu.SemaphoreType.DMA
    f32 = jnp.float32
    scores = pl.pallas_call(
        slot_kernel,
        out_shape=jax.ShapeDtypeStruct((slots, rows, columns), f32),
        in_specs=[
            pl.BlockSpec(memory_space=pl.ANY),
            pl.BlockSpec(memory_space=pl.ANY),
            pl.BlockSpec(memory_space=pltpu.SMEM),
        ],
        out_specs=pl.BlockSpec(memory_space=pl.ANY),
        scratch_shapes=[
            pltpu.VMEM((slots, rows, depth), slot.dtype),
            pltpu.VMEM((columns, depth), grads.dtype),
            pltpu.VMEM((depth, columns), grads.dtype),
            pltpu.VMEM((slots, 2, rows, columns // 2), f32),
            pltpu.VMEM((slots, rows, columns // 2), f32),
            pltpu.VMEM((slots, rows, columns // 2), f32),
            pltpu.VMEM((slots, rows, columns // 2), f32),
            pltpu.VMEM((slots, rows, columns // 2), f32),
            dma((2,)),
            dma((slots, chunks)),
            dma((slots, chunks)),
            dma((slots, chunks)),
            dma((slots, chunks)),
            dma((slots, chunks)),
            dma((items,)),
            dma((items,)),
            dma((items,)),
            dma((items,)),
            dma((items,)),
            dma((items,)),
            dma((items,)),
        ],
        compiler_params=pltpu.CompilerParams(
            collective_id=0, has_side_effects=True, vmem_limit_bytes=56 * 1024 * 1024
        ),
        cost_estimate=pl.CostEstimate(
            flops=2 * slots * rows * columns * depth, bytes_accessed=16 << 20, transcendentals=0
        ),
    )(grads, slot, lr_weights)
    return lax.dynamic_index_in_dim(scores, owners[lax.axis_index("ckpt")], 0, keepdims=False)


def solution(mesh):
    placed = (P("ckpt", ("parts", "dp"), None), P("ckpt", "dp", None, None), P(), P("ckpt"))
    sizes = dict(mesh.shape)
    every = sizes["dp"] == GROUPS and sizes["ckpt"] == GROUPS and sizes["parts"] == 2
    return jax.shard_map(
        all_slots_owned if every else per_device,
        mesh=mesh,
        in_specs=placed,
        out_specs=P("ckpt", ("parts", "dp")),
        check_vma=False,
    )
```
